32 devices in a mesh: grp: 2 (over y), ctx: 8 (over z, core), dp: 2 (over x).
Axes of the slice: x: 2, y: 2, z: 4, core: 2. Of those that a mesh axis runs over, the one named last changes fastest.
Arguments:
- resid: bfloat16 [2, 1024, 1024], P('dp', 'ctx'), may hold values from -6 to 6
- attn_ctx: bfloat16 [2, 1024, 1024], P('dp', 'ctx', 'grp'), may hold values from -6 to 6
- enc_out_weight: bfloat16 [1024, 1024], P('grp'), may hold values from -0.1875 to 0.1875
- enc_gain: bfloat16 [1024], replicated, may hold values from 0.25 to 1.75
- key_weight: bfloat16 [1024, 1024], P(None, 'grp'), may hold values from -0.1875 to 0.1875
- value_weight: bfloat16 [1024, 1024], P(None, 'grp'), may hold values from -0.1875 to 0.1875
- visual_grad: bfloat16 [2, 1024, 1024], P('dp', 'ctx'), may hold values from -6 to 6
- scene_lengths: int32 [2, 4], P('dp'), may hold values from 1 to 384, 1024 in all within a row
- text_queries: bfloat16 [2, 1280, 4096], P('dp', 'ctx', 'grp'), may hold values from -86 to 86
- text_segments: int32 [2, 1280], P('dp', 'ctx'), may hold values from 0 to 7, never falling along the last dimension, each value on 1 to 320 neighbouring positions
- doc_scene: int32 [2, 8], P('dp'), may hold values from 0 to 3
Outputs:
- cross_context: bfloat16 [2, 1280, 4096], P('dp', 'ctx', 'grp')
- enc_out_grad: float32 [1024, 1024], P(('grp', 'ctx'))
The draws below stay inside these ranges and needn't reach their ends.
Inputs may be any that keep to these rules, and one draw needn't show every extreme that they name: `scene_lengths`: each replica's counts sum to 1024; the largest is exactly the maximum. `text_segments`: never falling along a sequence.
All inputs are finite; a program needn't handle non-finite values.
Results may differ from the reference program's by a relative error of at most 0.025.
Values may be sent and summed in bfloat16 or wider, within the bound.
A program may use at most 64 MiB of HBM per device.

```python
import math
import jax
import jax.numpy as jnp
import numpy as np
from jax import lax

D_ENC = 1024
Q_HEADS = 32
KV_HEADS = 8
HEAD_DIM = 128
SCENES = 4
DOCS = 8
ENC_TOKENS = 1024
TEXT_TOKENS = 1280
N_DP = 2


def draw_text_queries(key, part):
    first_key = jax.random.fold_in(jax.random.fold_in(key, 17), 0)
    shape = (N_DP, TEXT_TOKENS, Q_HEADS * HEAD_DIM)
    values = jnp.clip(jax.random.normal(first_key, shape, jnp.float32), -6.0, 6.0)
    return values.astype(jnp.bfloat16)


def with_ends(drawn, rng, least, top_value):
    longest = drawn.shape.index(max(drawn.shape))
    spots = []
    for shift in (0, 1):
        where = [jax.random.randint(jax.random.fold_in(rng, axis), (), 0, length) for axis, length in enumerate(drawn.shape)]
        where[longest] = (where[longest] + shift) % drawn.shape[longest]
        spots.append(tuple(where))
    return drawn.at[spots[0]].set(least).at[spots[1]].set(top_value)


def with_spikes(drawn, key, source, target, blocks, factor):
    def block_of(dim):
        return (jnp.arange(drawn.shape[dim]) // (drawn.shape[dim] // blocks)).reshape((-1,) + (1,) * (drawn.ndim - 1 - dim))

    near = jax.random.permutation(key, blocks)[block_of(target)]
    other_side = (block_of(target) + blocks // 2) % blocks
    return jnp.where((block_of(source) == near) | (block_of(source) == other_side), factor * drawn, drawn)


def level_of(key, dims, cuts, least, high):
    def one(dim, parts):
        draws = jax.random.uniform(jax.random.fold_in(jax.random.fold_in(key, 6), dim), (parts,), jnp.float32, least / len(cuts), high / len(cuts))
        return jnp.repeat(jnp.exp(draws), dims[dim] // parts).reshape((-1,) + (1,) * (len(dims) - dim - 1))

    loudness = one(*cuts[0])
    for cut in cuts[1:]:
        loudness = loudness * one(*cut)
    return loudness


def length_profile(amount, total, bound, lean):
    loads = [(1 << 20) // math.isqrt(standing ** lean) + 1 for standing in range(2, amount + 1)]
    surplus, given = total - bound - (amount - 1), [1] * (amount - 1)
    while surplus > 0:
        movable = [i for i in range(amount - 1) if given[i] < bound]
        whole, remaining = sum([loads[i] for i in movable]), surplus
        for i in movable:
            more = min(bound - given[i], max(1, remaining * loads[i] // whole), surplus)
            given[i] = given[i] + more
            surplus = surplus - more
    return np.array([bound] + given)


def uneven_parts(stream_key, number_of, total, limit, skew):
    if number_of == 2:
        one = jax.random.randint(stream_key, (), max(1, total - limit), min(limit, total - 1) + 1)
        return jnp.stack([one, total - one])
    sizes = jnp.asarray(length_profile(number_of, total, limit, skew), jnp.int32)
    pairs = (number_of - 1) // 2
    donor, sink = sizes[1:1 + 2 * pairs:2], sizes[2:2 + 2 * pairs:2]
    margin = jnp.minimum(donor - 1, limit - sink)
    moved = jax.random.randint(jax.random.fold_in(stream_key, 1), (pairs,), 0, 1 << 20) % (margin + 1)
    sizes = sizes.at[1:1 + 2 * pairs:2].set(donor - moved).at[2:2 + 2 * pairs:2].set(sink + moved)
    return sizes[jax.random.permutation(jax.random.fold_in(stream_key, 2), number_of)]


def bell_draw(key, shape, width, limit, cuts=(), kind=jnp.bfloat16):
    values = jax.random.normal(key, shape, jnp.float32) * width
    if len(cuts) > 0:
        values = level_of(key, shape, cuts, -0.22, 0.18) * values
    return jnp.clip(values, min=-limit, max=limit).astype(kind)


def heavy_noise(key, extent, spread, most, pieces, heavy, kind=jnp.bfloat16):
    drawn = spread * jax.random.normal(key, extent, jnp.float32)
    if pieces:
        drawn = drawn * level_of(key, extent, pieces, -0.22, 0.18)
    return jnp.clip(with_spikes(drawn, jax.random.fold_in(key, 3), *heavy), -most, most).astype(kind)


def setup_inputs(seed: int = 0) -> dict:
    key_list = jax.random.split(jax.random.key(seed), 12)
    resid = bell_draw(key_list[0], (N_DP, ENC_TOKENS, D_ENC), 1.0, 6.0, ((0, 2), (1, 8)))
    attn_ctx = heavy_noise(key_list[1], (N_DP, ENC_TOKENS, D_ENC), 1.0, 6.0, ((0, 2), (1, 8), (2, 2)), (1, 2, 8, 2.0))
    enc_out_weight = bell_draw(key_list[2], (D_ENC, D_ENC), D_ENC ** -0.5, 0.1875, ((0, 2),))
    enc_gain = jnp.clip(1.0 + 0.15 * jax.random.normal(key_list[3], (D_ENC,), jnp.float32), 0.25, 1.75).astype(jnp.bfloat16)
    key_weight = bell_draw(key_list[4], (D_ENC, KV_HEADS * HEAD_DIM), D_ENC ** -0.5, 0.1875, ((1, 2),))
    value_weight = bell_draw(key_list[5], (D_ENC, KV_HEADS * HEAD_DIM), D_ENC ** -0.5, 0.1875, ((1, 2),))
    visual_grad = bell_draw(key_list[6], (N_DP, ENC_TOKENS, D_ENC), 1.0, 6.0, ((0, 2), (1, 8)))
    scene_lengths = jax.vmap(lambda own: uneven_parts(own, SCENES, ENC_TOKENS, ENC_TOKENS * 3 // 8, 2))(jax.random.split(key_list[7], N_DP)).reshape((N_DP, SCENES)).astype(jnp.int32)
    text_queries = draw_text_queries(jax.random.fold_in(key_list[11], 71), 0)
    text_segments = jax.vmap(lambda own: jnp.searchsorted(jnp.cumsum(uneven_parts(own, DOCS, TEXT_TOKENS, TEXT_TOKENS // 4, 2)), jnp.arange(TEXT_TOKENS), side="right"))(jax.random.split(key_list[9], N_DP)).reshape((N_DP, TEXT_TOKENS)).astype(jnp.int32)
    doc_scene = with_ends(jax.random.randint(key_list[10], (N_DP, DOCS), 0, SCENES), jax.random.fold_in(key_list[10], 1), 0, SCENES - 1).astype(jnp.int32)
    return dict(resid=resid, attn_ctx=attn_ctx, enc_out_weight=enc_out_weight, enc_gain=enc_gain, key_weight=key_weight, value_weight=value_weight, visual_grad=visual_grad, scene_lengths=scene_lengths, text_queries=text_queries, text_segments=text_segments, doc_scene=doc_scene)


NEGATIVE = -1e+30
EPSILON = 1e-05

def scene_index(lengths, first_row, count):
    scene_ends = jnp.cumsum(lengths)
    position = first_row + jnp.arange(count, dtype=jnp.int32)
    return lax.optimization_barrier(jnp.sum((position[:, None] >= scene_ends[None, :]).astype(jnp.int32), axis=1))

def query_scenes(segments, doc_scene):
    doc_numbers = jnp.arange(doc_scene.shape[0], dtype=jnp.int32)
    picked = (segments[:, None] == doc_numbers[None, :]).astype(jnp.int32)
    return lax.optimization_barrier(jnp.sum(picked * doc_scene[None, :], axis=1))

def normalize(hidden, enc_gain):
    root_mean = jnp.sqrt(lax.optimization_barrier(jnp.mean(hidden * hidden, axis=-1, keepdims=True)) + EPSILON)
    normed = hidden / root_mean
    visual = (normed * enc_gain.astype(jnp.float32)).astype(jnp.bfloat16)
    return (normed, root_mean, visual)

def norm_backward(cotangent, normed, root_mean, enc_gain):
    upstream = cotangent.astype(jnp.float32) * enc_gain.astype(jnp.float32)
    inner = lax.optimization_barrier(jnp.mean(upstream * normed, axis=-1, keepdims=True))
    return ((upstream - normed * inner) / root_mean).astype(jnp.bfloat16)

def attend(queries, key_rows, value_rows, query_scene, key_scene):
    group_size = Q_HEADS // KV_HEADS
    allowed = query_scene[:, None] == key_scene[None, :]

    def one_head(head_index):
        kv_index = head_index // group_size
        query_block = lax.dynamic_slice_in_dim(queries, head_index * HEAD_DIM, HEAD_DIM, 1)
        key_block = lax.dynamic_slice_in_dim(key_rows, kv_index * HEAD_DIM, HEAD_DIM, 1)
        value_block = lax.dynamic_slice_in_dim(value_rows, kv_index * HEAD_DIM, HEAD_DIM, 1)
        scores = jnp.dot(query_block, key_block.T, preferred_element_type=jnp.float32) * HEAD_DIM ** (-0.5)
        scores = jnp.where(allowed, scores, NEGATIVE)
        largest = lax.optimization_barrier(jnp.max(scores, axis=1, keepdims=True))
        weights = jnp.where(allowed, jnp.exp(scores - largest), 0.0).astype(jnp.bfloat16)
        totals = lax.optimization_barrier(jnp.sum(weights.astype(jnp.float32), axis=1, keepdims=True))
        result = jnp.dot(weights, value_block, preferred_element_type=jnp.float32) / totals
        return result.astype(jnp.bfloat16)
    stacked = lax.map(one_head, jnp.arange(Q_HEADS, dtype=jnp.int32))
    return jnp.transpose(stacked, (1, 0, 2)).reshape(queries.shape[0], Q_HEADS * HEAD_DIM)

def reference(resid, attn_ctx, enc_out_weight, enc_gain, key_weight, value_weight, visual_grad, scene_lengths, text_queries, text_segments, doc_scene):

    def replica(index):
        hidden = resid[index].astype(jnp.float32) + jnp.dot(attn_ctx[index], enc_out_weight, preferred_element_type=jnp.float32)
        normed, root_mean, visual = normalize(hidden, enc_gain)
        key_rows = jnp.dot(visual, key_weight, preferred_element_type=jnp.float32).astype(jnp.bfloat16)
        value_rows = jnp.dot(visual, value_weight, preferred_element_type=jnp.float32).astype(jnp.bfloat16)
        hidden_grad = norm_backward(visual_grad[index], normed, root_mean, enc_gain)
        weight_term = jnp.dot(attn_ctx[index].T, hidden_grad, preferred_element_type=jnp.float32)
        key_scene = scene_index(scene_lengths[index], jnp.int32(0), ENC_TOKENS)
        query_scene = query_scenes(text_segments[index], doc_scene[index])
        context = attend(text_queries[index], key_rows, value_rows, query_scene, key_scene)
        return (context, weight_term)
    contexts, weight_terms = lax.map(replica, jnp.arange(N_DP, dtype=jnp.int32))
    return (contexts, lax.optimization_barrier(jnp.sum(weight_terms, axis=0)))
```

```python
import functools
import math

import jax
import jax.numpy as jnp
from jax import lax
from jax.experimental import pallas as pl
from jax.experimental.pallas import tpu as pltpu
from jax.sharding import PartitionSpec as P

HEAD_DIM = 128
GROUP_SIZE = 4
MASKED = -2e30
START_MAX = -1e30
EPSILON = 1e-05
F32 = jnp.float32
BF16 = jnp.bfloat16
MESH = pl.DeviceIdType.MESH


def kernel(
    sizes,
    resid_hbm,
    ctx_hbm,
    wo_hbm,
    gain_ref,
    wk_hbm,
    wv_hbm,
    vgrad_hbm,
    lengths_ref,
    query_hbm,
    segment_ref,
    docs_ref,
    cross_ref,
    grad_ref,
    resid_v,
    ctx_v,
    wo_v,
    wk_v,
    wv_v,
    vgrad_v,
    query_v,
    part,
    y_out,
    y_in,
    visual,
    hid_grad,
    stacked,
    k_buf,
    v_buf,
    run_max,
    run_acc,
    scene_col,
    dw,
    dw_core,
    s1,
    dw_x,
    s2,
    dw_z,
    fin,
    fin_in,
    load_sem,
    y_sem,
    vz_sem,
    vy_sem,
    vc_sem,
    dc_sem,
    dx_sem,
    dz_sem,
    df_sem,
):
    n_ctx, n_dp = sizes
    nz = n_ctx // 2
    g = lax.axis_index("grp")
    c = lax.axis_index("ctx")
    r = lax.axis_index("dp")
    z, core = c // 2, c % 2
    half = resid_v.shape[1]
    features = resid_v.shape[2]
    kv_heads = k_buf.shape[0]
    text = query_v.shape[0]
    width = dw.shape[4]
    owner_rows = dw.shape[3]
    chunk = 4 * half

    y_id = (1 - g, c, r)
    core_id = (g, z * 2 + 1 - core, r)

    def z_to(k):
        return lax.rem(z + k, nz)

    def z_from(k):
        return lax.rem(z + nz - k, nz)

    def dp_to(j):
        return lax.rem(r + j, n_dp)

    def dp_from(j):
        return lax.rem(r + n_dp - j, n_dp)

    loads = []
    for i, (src, dst) in enumerate(
        (
            (ctx_hbm, ctx_v),
            (wo_hbm, wo_v),
            (resid_hbm, resid_v),
            (vgrad_hbm, vgrad_v),
            (wk_hbm, wk_v),
            (wv_hbm, wv_v),
            (query_hbm, query_v),
        )
    ):
        load = pltpu.make_async_copy(src, dst, load_sem.at[i])
        load.start()
        loads.append(load)

    barrier = pltpu.get_barrier_semaphore()
    peers = [y_id, core_id]
    peers += [(g, z_to(k) * 2 + core, r) for k in range(1, nz)]
    peers += [(g, c, dp_to(j)) for j in range(1, n_dp)]
    for peer in peers:
        pl.semaphore_signal(barrier, inc=1, device_id=peer, device_id_type=MESH)

    started = []

    def remote(src, dst, sem, device):
        return pltpu.make_async_remote_copy(
            src_ref=src,
            dst_ref=dst,
            send_sem=sem.at[0],
            recv_sem=sem.at[1],
            device_id=device,
            device_id_type=MESH,
        )

    def send(src, dst, sem, device):
        copy = remote(src, dst, sem, device)
        copy.start()
        started.append(copy)

    def arrived(dst, sem, device):
        remote(dst, dst, sem, device).wait_recv()

    loads[0].wait()
    loads[1].wait()
    product = jnp.dot(ctx_v[...], wo_v[...], preferred_element_type=F32)
    part[...] = product.reshape(part.shape)
    y_out[...] = product.astype(BF16).reshape(y_out.shape)
    pl.semaphore_wait(barrier, len(peers))
    for i, h in enumerate((1 - g, g)):
        send(y_out.at[h], y_in.at[h], y_sem.at[i], y_id)

    segment_row = segment_ref[...].astype(F32)
    on_diagonal = lax.broadcasted_iota(jnp.int32, (text, text), 0) == lax.broadcasted_iota(
        jnp.int32, (text, text), 1
    )
    segment_col = jnp.sum(jnp.where(on_diagonal, segment_row, 0.0), axis=1, keepdims=True)
    scene = jnp.zeros((text, 1), F32)
    for d in range(docs_ref.shape[1]):
        scene = scene + jnp.where(segment_col == d, docs_ref[0, d].astype(F32), 0.0)
    scene_col[...] = jnp.broadcast_to(scene, scene_col.shape)

    run_max[...] = jnp.full(run_max.shape, START_MAX, F32)
    run_acc[...] = jnp.zeros(run_acc.shape, F32)
    for head in range(kv_heads):
        v_buf[head, :, HEAD_DIM:] = jnp.ones((chunk, HEAD_DIM), BF16)

    gain = gain_ref[...].astype(F32)
    loads[2].wait()
    loads[3].wait()

    def normalize(h):
        hidden = resid_v[h].astype(F32) + part[h] + y_in[h].astype(F32)
        inverse = lax.rsqrt(jnp.mean(hidden * hidden, axis=-1, keepdims=True) + EPSILON)
        normed = hidden * inverse
        visual[c * 2 + h] = (normed * gain).astype(BF16)
        return normed, inverse

    def backward(h, normed, inverse):
        upstream = vgrad_v[h].astype(F32) * gain
        inner = jnp.mean(upstream * normed, axis=-1, keepdims=True)
        hid_grad[h] = ((upstream - normed * inner) * inverse).astype(BF16)

    arrived(y_in.at[g], y_sem.at[0], y_id)
    saved = normalize(g)
    mine = visual.at[c * 2 + g]
    for k in range(1, nz):
        send(mine, mine, vz_sem.at[k], (g, z_to(k) * 2 + core, r))
    send(mine, mine, vc_sem.at[0, 0], core_id)
    backward(g, *saved)
    arrived(y_in.at[1 - g], y_sem.at[1], y_id)
    saved = normalize(1 - g)
    other = visual.at[c * 2 + 1 - g]
    send(other, other, vc_sem.at[0, 1], core_id)
    backward(1 - g, *saved)

    grads = hid_grad[...].reshape(2 * half, features)
    step = min(HEAD_DIM, ctx_v.shape[1])
    for first in range(0, ctx_v.shape[1], step):
        term = lax.dot_general(
            ctx_v[:, first : first + step],
            grads,
            (((0,), (0,)), ((), ())),
            preferred_element_type=F32,
        ).astype(BF16)
        for low in range(0, step, owner_rows):
            owner = (first + low) // owner_rows
            for j in range(n_dp):
                dw[owner % 2, j, owner // 2] = term[
                    low : low + owner_rows, j * width : (j + 1) * width
                ]
    send(dw.at[1 - core], dw_core, dc_sem, core_id)

    loads[4].wait()
    loads[5].wait()
    loads[6].wait()
    for head in range(kv_heads):
        for member in range(GROUP_SIZE):
            column = (head * GROUP_SIZE + member) * HEAD_DIM
            stacked[head, member * text : (member + 1) * text, :] = query_v[
                :, column : column + HEAD_DIM
            ]

    score_scale = HEAD_DIM ** (-0.5) * math.log2(math.e)

    def absorb(k):
        source = z_from(k)
        mine_id, their_id = source * 2 + core, source * 2 + 1 - core
        arrived(visual.at[their_id * 2 + g], vc_sem.at[k, 0], core_id)
        arrived(visual.at[their_id * 2 + 1 - g], vc_sem.at[k, 1], core_id)
        rows = visual[pl.ds(source * 4, 4)].reshape(chunk, features)
        keys = jnp.dot(rows, wk_v[...], preferred_element_type=F32).astype(BF16)
        values = jnp.dot(rows, wv_v[...], preferred_element_type=F32).astype(BF16)
        for head in range(kv_heads):
            k_buf[head] = keys[:, head * HEAD_DIM : (head + 1) * HEAD_DIM]
            v_buf[head, :, :HEAD_DIM] = values[:, head * HEAD_DIM : (head + 1) * HEAD_DIM]
        position = source * chunk + lax.broadcasted_iota(jnp.int32, (1, chunk), 1)
        key_scene = jnp.zeros((1, chunk), F32)
        end = lengths_ref[0, 0]
        for s in range(lengths_ref.shape[1]):
            key_scene = key_scene + jnp.where(position >= end, 1.0, 0.0)
            if s + 1 < lengths_ref.shape[1]:
                end = end + lengths_ref[0, s + 1]
        allowed = scene_col[:, :1] == key_scene

        def one_head(head):
            scores = lax.dot_general(
                stacked[head], k_buf[head], (((1,), (1,)), ((), ())), preferred_element_type=F32
            )
            scores = scores.reshape(GROUP_SIZE, text, chunk) * score_scale
            scores = jnp.where(allowed[None], scores, MASKED).reshape(GROUP_SIZE * text, chunk)
            old_max = run_max[head][:, :1]
            new_max = jnp.maximum(old_max, jnp.max(scores, axis=1, keepdims=True))
            weights = jnp.exp2(scores - new_max).astype(BF16)
            added = jnp.dot(weights, v_buf[head], preferred_element_type=F32)
            run_acc[head] = run_acc[head] * jnp.exp2(old_max - new_max) + added
            run_max[head] = jnp.broadcast_to(new_max, run_max.shape[1:])

        if nz <= 4:
            for head in range(kv_heads):
                one_head(head)
        else:
            pl.loop(0, kv_heads)(one_head)

    def z_relay(k):
        block = visual.at[(z_from(k) * 2 + core) * 2 + g]
        arrived(block, vz_sem.at[k], y_id)
        send(block, block, vy_sem.at[k], y_id)
        send(block, block, vc_sem.at[k, 0], core_id)

    def y_relay(k):
        block = visual.at[(z_from(k) * 2 + core) * 2 + 1 - g]
        arrived(block, vy_sem.at[k], y_id)
        send(block, block, vc_sem.at[k, 1], core_id)

    def grad_dp():
        arrived(dw_core, dc_sem, core_id)
        s1[...] = (dw[core].astype(F32) + dw_core[...].astype(F32)).astype(BF16)
        for j in range(1, n_dp):
            send(s1.at[dp_to(j)], dw_x.at[j], dx_sem.at[j], (g, c, dp_to(j)))

    def grad_z():
        total = s1[r].astype(F32)
        for j in range(1, n_dp):
            arrived(dw_x.at[j], dx_sem.at[j], (g, c, dp_to(j)))
            total = total + dw_x[j].astype(F32)
        s2[...] = total.astype(BF16)
        for k in range(1, nz):
            send(s2.at[z_to(k)], dw_z.at[k], dz_sem.at[k], (g, z_to(k) * 2 + core, r))

    def grad_final():
        total = s2[z].astype(F32)
        for k in range(1, nz):
            arrived(dw_z.at[k], dz_sem.at[k], (g, z_to(k) * 2 + core, r))
            total = total + dw_z[k].astype(F32)
        fin[...] = total.astype(BF16)
        for j in range(1, n_dp):
            send(fin, fin_in.at[j], df_sem.at[j], (g, c, dp_to(j)))

    grad_dp()
    absorb(0)
    for k in range(1, nz):
        z_relay(k)
        if k == 1:
            grad_z()
        if k >= 2:
            y_relay(k - 1)
        if k >= 3:
            absorb(k - 2)
    y_relay(nz - 1)
    if nz > 2:
        absorb(nz - 2)
    grad_final()
    absorb(nz - 1)

    for head in range(kv_heads):
        result = (run_acc[head][:, :HEAD_DIM] / run_acc[head][:, HEAD_DIM:]).astype(BF16)
        for member in range(GROUP_SIZE):
            column = (head * GROUP_SIZE + member) * HEAD_DIM
            cross_ref[:, column : column + HEAD_DIM] = result[member * text : (member + 1) * text]

    def columns(owner):
        return pl.ds(pl.multiple_of(owner * width, 128), width)

    grad_ref[:, columns(r)] = fin[...].astype(F32)
    for j in range(1, n_dp):
        arrived(fin_in.at[j], df_sem.at[j], (g, c, dp_to(j)))
        grad_ref[:, columns(dp_from(j))] = fin_in[j].astype(F32)

    for copy in started:
        copy.wait_send()


def local(
    n_ctx,
    n_dp,
    resid,
    attn_ctx,
    enc_out_weight,
    enc_gain,
    key_weight,
    value_weight,
    visual_grad,
    scene_lengths,
    text_queries,
    text_segments,
    doc_scene,
):
    rows, features = resid.shape[1:]
    half = rows // 2
    mine = attn_ctx.shape[2]
    text, query_width = text_queries.shape[1:]
    kv_width = key_weight.shape[1]
    kv_heads = kv_width // HEAD_DIM
    nz = n_ctx // 2
    owner_rows = mine // n_ctx
    width = features // n_dp
    chunk = 4 * half
    stacked = GROUP_SIZE * text
    hbm = pl.BlockSpec(memory_space=pl.ANY)
    vmem = pl.BlockSpec(memory_space=pltpu.VMEM)
    smem = pl.BlockSpec(memory_space=pltpu.SMEM)
    sem = pltpu.SemaphoreType.DMA
    halves = (2, half, features)
    cross, grad = pl.pallas_call(
        functools.partial(kernel, (n_ctx, n_dp)),
        out_shape=(
            jax.ShapeDtypeStruct((text, query_width), BF16),
            jax.ShapeDtypeStruct((owner_rows, features), F32),
        ),
        in_specs=[hbm, hbm, hbm, vmem, hbm, hbm, hbm, smem, hbm, vmem, smem],
        out_specs=(vmem, vmem),
        scratch_shapes=[
            pltpu.VMEM(halves, BF16),
            pltpu.VMEM((rows, mine), BF16),
            pltpu.VMEM((mine, features), BF16),
            pltpu.VMEM((features, kv_width), BF16),
            pltpu.VMEM((features, kv_width), BF16),
            pltpu.VMEM(halves, BF16),
            pltpu.VMEM((text, query_width), BF16),
            pltpu.VMEM(halves, F32),
            pltpu.VMEM(halves, BF16),
            pltpu.VMEM(halves, BF16),
            pltpu.VMEM((2 * n_ctx, half, features), BF16),
            pltpu.VMEM(halves, BF16),
            pltpu.VMEM((kv_heads, stacked, HEAD_DIM), BF16),
            pltpu.VMEM((kv_heads, chunk, HEAD_DIM), BF16),
            pltpu.VMEM((kv_heads, chunk, 2 * HEAD_DIM), BF16),
            pltpu.VMEM((kv_heads, stacked, HEAD_DIM), F32),
            pltpu.VMEM((kv_heads, stacked, 2 * HEAD_DIM), F32),
            pltpu.VMEM((text, HEAD_DIM), F32),
            pltpu.VMEM((2, n_dp, nz, owner_rows, width), BF16),
            pltpu.VMEM((n_dp, nz, owner_rows, width), BF16),
            pltpu.VMEM((n_dp, nz, owner_rows, width), BF16),
            pltpu.VMEM((n_dp, nz, owner_rows, width), BF16),
            pltpu.VMEM((nz, owner_rows, width), BF16),
            pltpu.VMEM((nz, owner_rows, width), BF16),
            pltpu.VMEM((owner_rows, width), BF16),
            pltpu.VMEM((n_dp, owner_rows, width), BF16),
            sem((7,)),
            sem((2, 2)),
            sem((nz, 2)),
            sem((nz, 2)),
            sem((nz, 2, 2)),
            sem((2,)),
            sem((n_dp, 2)),
            sem((nz, 2)),
            sem((n_dp, 2)),
        ],
        compiler_params=pltpu.CompilerParams(
            collective_id=0, has_side_effects=True, vmem_limit_bytes=56 * 1024 * 1024
        ),
        name="encoder_cross",
    )(
        resid.reshape(halves),
        attn_ctx.reshape(rows, mine),
        enc_out_weight,
        enc_gain.reshape(1, features),
        key_weight,
        value_weight,
        visual_grad.reshape(halves),
        scene_lengths,
        text_queries.reshape(text, query_width),
        text_segments,
        doc_scene,
    )
    return cross[None], grad


def solution(mesh):
    in_specs = (
        P("dp", "ctx", None),
        P("dp", "ctx", "grp"),
        P("grp", None),
        P(),
        P(None, "grp"),
        P(None, "grp"),
        P("dp", "ctx", None),
        P("dp", None),
        P("dp", "ctx", "grp"),
        P("dp", "ctx"),
        P("dp", None),
    )
    out_specs = (P("dp", "ctx", "grp"), P(("grp", "ctx"), None))
    return jax.shard_map(
        functools.partial(local, mesh.shape["ctx"], mesh.shape["dp"]),
        mesh=mesh,
        in_specs=in_specs,
        out_specs=out_specs,
        check_vma=False,
    )
```

```python
import functools
import math

import jax
import jax.numpy as jnp
from jax import lax
from jax.experimental import pallas as pl
from jax.experimental.pallas import tpu as pltpu
from jax.sharding import PartitionSpec as P

HEAD_DIM = 128
GROUP_SIZE = 4
MASKED = -2e30
START_MAX = -1e30
EPSILON = 1e-05
F32 = jnp.float32
BF16 = jnp.bfloat16
MESH = pl.DeviceIdType.MESH


def kernel(
    sizes,
    resid_hbm,
    ctx_hbm,
    wo_hbm,
    gain_ref,
    wk_hbm,
    wv_hbm,
    vgrad_hbm,
    lengths_ref,
    query_hbm,
    segment_ref,
    docs_ref,
    cross_ref,
    grad_ref,
    resid_v,
    ctx_v,
    wo_v,
    wk_v,
    wv_v,
    vgrad_v,
    query_v,
    part,
    y_out,
    y_in,
    visual,
    hid_grad,
    stacked,
    k_buf,
    v_buf,
    run_max,
    run_acc,
    scene_row,
    bias,
    dw,
    dw_core,
    s1,
    dw_x,
    s2,
    dw_z,
    fin,
    fin_in,
    load_sem,
    y_sem,
    vz_sem,
    vy_sem,
    vc_sem,
    dc_sem,
    dx_sem,
    dz_sem,
    df_sem,
):
    n_ctx, n_dp = sizes
    nz = n_ctx // 2
    g = lax.axis_index("grp")
    c = lax.axis_index("ctx")
    r = lax.axis_index("dp")
    z, core = c // 2, c % 2
    half = resid_v.shape[1]
    features = resid_v.shape[2]
    kv_heads = k_buf.shape[0]
    text = query_v.shape[0]
    width = dw.shape[4]
    owner_rows = dw.shape[3]
    chunk = 4 * half

    y_id = (1 - g, c, r)
    core_id = (g, z * 2 + 1 - core, r)

    def z_to(k):
        return lax.rem(z + k, nz)

    def z_from(k):
        return lax.rem(z + nz - k, nz)

    def dp_to(j):
        return lax.rem(r + j, n_dp)

    def dp_from(j):
        return lax.rem(r + n_dp - j, n_dp)

    loads = []
    for i, (src, dst) in enumerate(
        (
            (ctx_hbm, ctx_v),
            (wo_hbm, wo_v),
            (resid_hbm, resid_v),
            (vgrad_hbm, vgrad_v),
            (wk_hbm, wk_v),
            (wv_hbm, wv_v),
            (query_hbm, query_v),
        )
    ):
        loads.append(pltpu.make_async_copy(src, dst, load_sem.at[i]))
    for load in loads[:3]:
        load.start()

    barrier = pltpu.get_barrier_semaphore()
    peers = [y_id, core_id]
    peers += [(g, z_to(k) * 2 + core, r) for k in range(1, nz)]
    peers += [(g, c, dp_to(j)) for j in range(1, n_dp)]
    for peer in peers:
        pl.semaphore_signal(barrier, inc=1, device_id=peer, device_id_type=MESH)

    started = []

    def remote(src, dst, sem, device):
        return pltpu.make_async_remote_copy(
            src_ref=src,
            dst_ref=dst,
            send_sem=sem.at[0],
            recv_sem=sem.at[1],
            device_id=device,
            device_id_type=MESH,
        )

    def send(src, dst, sem, device):
        copy = remote(src, dst, sem, device)
        copy.start()
        started.append(copy)

    def arrived(dst, sem, device):
        remote(dst, dst, sem, device).wait_recv()

    loads[0].wait()
    loads[1].wait()
    for load in loads[3:]:
        load.start()
    product = jnp.dot(ctx_v[...], wo_v[...], preferred_element_type=F32)
    part[...] = product.reshape(part.shape)
    y_out[...] = product.astype(BF16).reshape(y_out.shape)
    pl.semaphore_wait(barrier, len(peers))
    for i, h in enumerate((1 - g, g)):
        send(y_out.at[h], y_in.at[h], y_sem.at[i], y_id)

    scene = jnp.zeros((1, text), F32)
    for d in range(docs_ref.shape[1]):
        scene = scene + jnp.where(segment_ref[...] == d, docs_ref[0, d].astype(F32), 0.0)
    scene_row[...] = jnp.concatenate([scene] * GROUP_SIZE, axis=1)

    run_max[...] = jnp.full(run_max.shape, START_MAX, F32)
    run_acc[...] = jnp.zeros(run_acc.shape, F32)
    for head in range(kv_heads):
        v_buf[head, HEAD_DIM:, :] = jnp.ones((v_buf.shape[1] - HEAD_DIM, chunk), BF16)

    gain = gain_ref[...].astype(F32).reshape(1, features)
    loads[2].wait()
    loads[3].wait()

    def normalize(h):
        hidden = resid_v[h].astype(F32) + part[h] + y_in[h].astype(F32)
        inverse = lax.rsqrt(jnp.mean(hidden * hidden, axis=-1, keepdims=True) + EPSILON)
        normed = hidden * inverse
        visual[c * 2 + h] = (normed * gain).astype(BF16)
        return normed, inverse

    def backward(h, normed, inverse):
        upstream = vgrad_v[h].astype(F32) * gain
        inner = jnp.mean(upstream * normed, axis=-1, keepdims=True)
        hid_grad[h] = ((upstream - normed * inner) * inverse).astype(BF16)

    arrived(y_in.at[g], y_sem.at[0], y_id)
    saved = normalize(g)
    mine = visual.at[c * 2 + g]
    for k in range(1, nz):
        send(mine, mine, vz_sem.at[k], (g, z_to(k) * 2 + core, r))
    send(mine, mine, vc_sem.at[0, 0], core_id)
    backward(g, *saved)
    arrived(y_in.at[1 - g], y_sem.at[1], y_id)
    saved = normalize(1 - g)
    other = visual.at[c * 2 + 1 - g]
    send(other, other, vc_sem.at[0, 1], core_id)
    backward(1 - g, *saved)

    grads = hid_grad[...].reshape(2 * half, features)
    step = min(HEAD_DIM, ctx_v.shape[1])
    for first in range(0, ctx_v.shape[1], step):
        term = lax.dot_general(
            ctx_v[:, first : first + step],
            grads,
            (((0,), (0,)), ((), ())),
            preferred_element_type=F32,
        ).astype(BF16)
        for low in range(0, step, owner_rows):
            owner = (first + low) // owner_rows
            for j in range(n_dp):
                dw[owner % 2, j, owner // 2] = term[
                    low : low + owner_rows, j * width : (j + 1) * width
                ]
    send(dw.at[1 - core], dw_core, dc_sem, core_id)

    loads[4].wait()
    loads[5].wait()
    loads[6].wait()
    for head in range(kv_heads):
        for member in range(GROUP_SIZE):
            column = (head * GROUP_SIZE + member) * HEAD_DIM
            stacked[head, member * text : (member + 1) * text, :] = query_v[
                :, column : column + HEAD_DIM
            ]

    score_scale = HEAD_DIM ** (-0.5) * math.log2(math.e)

    def absorb(k):
        source = z_from(k)
        mine_id, their_id = source * 2 + core, source * 2 + 1 - core
        arrived(visual.at[their_id * 2 + g], vc_sem.at[k, 0], core_id)
        arrived(visual.at[their_id * 2 + 1 - g], vc_sem.at[k, 1], core_id)
        rows = visual[pl.ds(source * 4, 4)].reshape(chunk, features)
        keys = jnp.dot(rows, wk_v[...], preferred_element_type=F32).astype(BF16)
        values = jnp.dot(rows, wv_v[...], preferred_element_type=F32).T.astype(BF16)
        for head in range(kv_heads):
            k_buf[head] = keys[:, head * HEAD_DIM : (head + 1) * HEAD_DIM]
            v_buf[head, :HEAD_DIM, :] = values[head * HEAD_DIM : (head + 1) * HEAD_DIM]
        position = source * chunk + lax.broadcasted_iota(jnp.int32, (chunk, 1), 0)
        key_scene = jnp.zeros((chunk, 1), F32)
        end = lengths_ref[0, 0]
        for s in range(lengths_ref.shape[1]):
            key_scene = key_scene + jnp.where(position >= end, 1.0, 0.0)
            if s + 1 < lengths_ref.shape[1]:
                end = end + lengths_ref[0, s + 1]
        bias[...] = jnp.where(key_scene == scene_row[...], 0.0, MASKED)

        def one_head(head):
            scores = lax.dot_general(
                k_buf[head], stacked[head], (((1,), (1,)), ((), ())), preferred_element_type=F32
            )
            scores = scores * score_scale + bias[...]
            old_max = run_max[head]
            new_max = jnp.maximum(old_max, jnp.max(scores, axis=0, keepdims=True))
            weights = jnp.exp2(scores - new_max).astype(BF16)
            added = jnp.dot(v_buf[head], weights, preferred_element_type=F32)
            run_acc[head] = run_acc[head] * jnp.exp2(old_max - new_max) + added
            run_max[head] = new_max

        if nz <= 4:
            for head in range(kv_heads):
                one_head(head)
        else:
            pl.loop(0, kv_heads)(one_head)

    def z_relay(k):
        block = visual.at[(z_from(k) * 2 + core) * 2 + g]
        arrived(block, vz_sem.at[k], y_id)
        send(block, block, vy_sem.at[k], y_id)
        send(block, block, vc_sem.at[k, 0], core_id)

    def y_relay(k):
        block = visual.at[(z_from(k) * 2 + core) * 2 + 1 - g]
        arrived(block, vy_sem.at[k], y_id)
        send(block, block, vc_sem.at[k, 1], core_id)

    def grad_dp():
        arrived(dw_core, dc_sem, core_id)
        s1[...] = (dw[core].astype(F32) + dw_core[...].astype(F32)).astype(BF16)
        for j in range(1, n_dp):
            send(s1.at[dp_to(j)], dw_x.at[j], dx_sem.at[j], (g, c, dp_to(j)))

    def grad_z():
        total = s1[r].astype(F32)
        for j in range(1, n_dp):
            arrived(dw_x.at[j], dx_sem.at[j], (g, c, dp_to(j)))
            total = total + dw_x[j].astype(F32)
        s2[...] = total.astype(BF16)
        for k in range(1, nz):
            send(s2.at[z_to(k)], dw_z.at[k], dz_sem.at[k], (g, z_to(k) * 2 + core, r))

    def grad_final():
        total = s2[z].astype(F32)
        for k in range(1, nz):
            arrived(dw_z.at[k], dz_sem.at[k], (g, z_to(k) * 2 + core, r))
            total = total + dw_z[k].astype(F32)
        fin[...] = total.astype(BF16)
        for j in range(1, n_dp):
            send(fin, fin_in.at[j], df_sem.at[j], (g, c, dp_to(j)))

    grad_dp()
    absorb(0)
    for k in range(1, nz):
        z_relay(k)
        if k == 1:
            grad_z()
        if k >= 2:
            y_relay(k - 1)
        if k >= 3:
            absorb(k - 2)
    y_relay(nz - 1)
    if nz > 2:
        absorb(nz - 2)
    grad_final()
    absorb(nz - 1)

    for head in range(kv_heads):
        total = run_acc[head]
        result = (total[:HEAD_DIM] / total[HEAD_DIM : HEAD_DIM + 1]).T.astype(BF16)
        for member in range(GROUP_SIZE):
            column = (head * GROUP_SIZE + member) * HEAD_DIM
            cross_ref[:, column : column + HEAD_DIM] = result[member * text : (member + 1) * text]

    def columns(owner):
        return pl.ds(pl.multiple_of(owner * width, 128), width)

    grad_ref[:, columns(r)] = fin[...].astype(F32)
    for j in range(1, n_dp):
        arrived(fin_in.at[j], df_sem.at[j], (g, c, dp_to(j)))
        grad_ref[:, columns(dp_from(j))] = fin_in[j].astype(F32)

    for copy in started:
        copy.wait_send()


def local(
    n_ctx,
    n_dp,
    resid,
    attn_ctx,
    enc_out_weight,
    enc_gain,
    key_weight,
    value_weight,
    visual_grad,
    scene_lengths,
    text_queries,
    text_segments,
    doc_scene,
):
    rows, features = resid.shape[1:]
    half = rows // 2
    mine = attn_ctx.shape[2]
    text, query_width = text_queries.shape[1:]
    kv_width = key_weight.shape[1]
    kv_heads = kv_width // HEAD_DIM
    nz = n_ctx // 2
    owner_rows = mine // n_ctx
    width = features // n_dp
    chunk = 4 * half
    stacked = GROUP_SIZE * text
    hbm = pl.BlockSpec(memory_space=pl.ANY)
    vmem = pl.BlockSpec(memory_space=pltpu.VMEM)
    smem = pl.BlockSpec(memory_space=pltpu.SMEM)
    sem = pltpu.SemaphoreType.DMA
    halves = (2, half, features)
    cross, grad = pl.pallas_call(
        functools.partial(kernel, (n_ctx, n_dp)),
        out_shape=(
            jax.ShapeDtypeStruct((text, query_width), BF16),
            jax.ShapeDtypeStruct((owner_rows, features), F32),
        ),
        in_specs=[hbm, hbm, hbm, vmem, hbm, hbm, hbm, smem, hbm, vmem, smem],
        out_specs=(vmem, vmem),
        scratch_shapes=[
            pltpu.VMEM(halves, BF16),
            pltpu.VMEM((rows, mine), BF16),
            pltpu.VMEM((mine, features), BF16),
            pltpu.VMEM((features, kv_width), BF16),
            pltpu.VMEM((features, kv_width), BF16),
            pltpu.VMEM(halves, BF16),
            pltpu.VMEM((text, query_width), BF16),
            pltpu.VMEM(halves, F32),
            pltpu.VMEM(halves, BF16),
            pltpu.VMEM(halves, BF16),
            pltpu.VMEM((2 * n_ctx, half, features), BF16),
            pltpu.VMEM(halves, BF16),
            pltpu.VMEM((kv_heads, stacked, HEAD_DIM), BF16),
            pltpu.VMEM((kv_heads, chunk, HEAD_DIM), BF16),
            pltpu.VMEM((kv_heads, HEAD_DIM + 16, chunk), BF16),
            pltpu.VMEM((kv_heads, 1, stacked), F32),
            pltpu.VMEM((kv_heads, HEAD_DIM + 16, stacked), F32),
            pltpu.VMEM((1, stacked), F32),
            pltpu.VMEM((chunk, stacked), F32),
            pltpu.VMEM((2, n_dp, nz, owner_rows, width), BF16),
            pltpu.VMEM((n_dp, nz, owner_rows, width), BF16),
            pltpu.VMEM((n_dp, nz, owner_rows, width), BF16),
            pltpu.VMEM((n_dp, nz, owner_rows, width), BF16),
            pltpu.VMEM((nz, owner_rows, width), BF16),
            pltpu.VMEM((nz, owner_rows, width), BF16),
            pltpu.VMEM((owner_rows, width), BF16),
            pltpu.VMEM((n_dp, owner_rows, width), BF16),
            sem((7,)),
            sem((2, 2)),
            sem((nz, 2)),
            sem((nz, 2)),
            sem((nz, 2, 2)),
            sem((2,)),
            sem((n_dp, 2)),
            sem((nz, 2)),
            sem((n_dp, 2)),
        ],
        compiler_params=pltpu.CompilerParams(
            collective_id=0, has_side_effects=True, vmem_limit_bytes=56 * 1024 * 1024
        ),
        name="encoder_cross",
    )(
        resid.reshape(halves),
        attn_ctx.reshape(rows, mine),
        enc_out_weight,
        enc_gain,
        key_weight,
        value_weight,
        visual_grad.reshape(halves),
        scene_lengths,
        text_queries.reshape(text, query_width),
        text_segments,
        doc_scene,
    )
    return cross[None], grad


def solution(mesh):
    in_specs = (
        P("dp", "ctx", None),
        P("dp", "ctx", "grp"),
        P("grp", None),
        P(),
        P(None, "grp"),
        P(None, "grp"),
        P("dp", "ctx", None),
        P("dp", None),
        P("dp", "ctx", "grp"),
        P("dp", "ctx"),
        P("dp", None),
    )
    out_specs = (P("dp", "ctx", "grp"), P(("grp", "ctx"), None))
    return jax.shard_map(
        functools.partial(local, mesh.shape["ctx"], mesh.shape["dp"]),
        mesh=mesh,
        in_specs=in_specs,
        out_specs=out_specs,
        check_vma=False,
    )
```
